32 devices in a mesh: seq: 4 (over y, x), head: 8 (over z, core).
Axes of the slice: x: 2, y: 2, z: 4, core: 2. Of those that a mesh axis runs over, the one named last changes fastest.
Arguments:
- layer_input: bfloat16 [8192, 2048], P(('seq', 'head')), may hold values from -6 to 6
- mem_count: int32 [4], P('seq'), may hold values from 0 to 150, as said below
- text_len: int32 [4], P('seq'), may hold values from 924 to 1848
- slot_count: int32 [4], P('seq'), may hold values from 1 to 50
- w_query: bfloat16 [2048, 2048], P(None, 'head'), may hold values from -0.125 to 0.125
- w_key: bfloat16 [2048, 2048], P(None, 'head'), may hold values from -0.125 to 0.125
- w_value: bfloat16 [2048, 2048], P(None, 'head'), may hold values from -0.125 to 0.125
- b_query: bfloat16 [2048], P('head'), may hold values from -2 to 2
- b_value: bfloat16 [2048], P('head'), may hold values from -0.29882812 to 0.29882812
- ln1_gain: bfloat16 [2048], P(('seq', 'head')), may hold values from 0.5 to 1.5
- ln1_bias: bfloat16 [2048], P(('seq', 'head')), may hold values from -2 to 2
- w_out: bfloat16 [2048, 2048], P(('seq', 'head')), may hold values from -1 to 1
- b_out: bfloat16 [2048], P(('seq', 'head')), may hold values from -2 to 2
- ln2_gain: bfloat16 [2048], P(('seq', 'head')), may hold values from 0.5 to 1.5
- ln2_bias: bfloat16 [2048], P(('seq', 'head')), may hold values from -2 to 2
- w_up: bfloat16 [2048, 8192], P(None, ('seq', 'head')), may hold values from -0.125 to 0.125
- b_up: bfloat16 [8192], P(('seq', 'head')), may hold values from -3 to 3
- w_down: bfloat16 [8192, 2048], P(('seq', 'head')), may hold values from -0.0625 to 0.0625
- b_down: bfloat16 [2048], P(('seq', 'head')), may hold values from -2 to 2
- cotangent: bfloat16 [8192, 2048], P(('seq', 'head')), may hold values from -6 to 6
Outputs:
- out: bfloat16 [8192, 2048], P(('seq', 'head'))
- grad_input: bfloat16 [8192, 2048], P(('seq', 'head'))
- grad_w_query: float32 [2048, 2048], P(None, 'head')
- grad_w_key: float32 [2048, 2048], P(None, 'head')
- grad_w_value: float32 [2048, 2048], P(None, 'head')
- grad_b_query: float32 [2048], P('head')
- grad_b_value: float32 [2048], P('head')
- grad_ln1_gain: float32 [2048], P(('seq', 'head'))
- grad_ln1_bias: float32 [2048], P(('seq', 'head'))
- grad_w_out: float32 [2048, 2048], P(('seq', 'head'))
- grad_b_out: float32 [2048], P(('seq', 'head'))
- grad_ln2_gain: float32 [2048], P(('seq', 'head'))
- grad_ln2_bias: float32 [2048], P(('seq', 'head'))
- grad_w_up: float32 [2048, 8192], P(None, ('seq', 'head'))
- grad_b_up: float32 [8192], P(('seq', 'head'))
- grad_w_down: float32 [8192, 2048], P(('seq', 'head'))
- grad_b_down: float32 [2048], P(('seq', 'head'))
The draws below stay inside these ranges and needn't reach their ends.
Inputs may be any that keep to these rules, and one draw needn't show every extreme that they name: `mem_count`: one sequence has 150 memories, 1848 text positions and 50 summary slots.
All inputs are finite; a program needn't handle non-finite values.
Results may differ from the reference program's by a relative error of at most 0.017.
Values may be sent and summed in bfloat16 or wider, within the bound.
No kernel may reach another device: no remote copies, remote signals or barrier semaphores. Data moves between devices by JAX's collectives and lax.ppermute only.
A program may use at most 384 MiB of HBM per device.

```python
import jax
import jax.numpy as jnp
from jax import lax

D = 2048
HEADS = 32
HEAD_DIM = 64
FF = 8192
LENGTH = 2048
MEM = 150
SLOTS = 50
TEXT = 1848
SEQS = 4
TOKENS = 8192


def chosen_row(key):
    return jnp.arange(SEQS) == jax.random.randint(key, (), 0, SEQS)


def draw_mem_count(key, part):
    chosen = chosen_row(key)
    key = jax.random.fold_in(key, 11)
    sampled = jax.random.randint(key, (SEQS,), 0, MEM + 1)
    return jnp.where(chosen, MEM, sampled).astype(jnp.int32)


def draw_text_len(key, part):
    chosen = chosen_row(key)
    key = jax.random.fold_in(key, 12)
    sampled = jax.random.randint(key, (SEQS,), TEXT // 2, TEXT + 1)
    return jnp.where(chosen, TEXT, sampled).astype(jnp.int32)


def draw_slot_count(key, part):
    chosen = chosen_row(key)
    key = jax.random.fold_in(key, 13)
    sampled = jax.random.randint(key, (SEQS,), 1, SLOTS + 1)
    return jnp.where(chosen, SLOTS, sampled).astype(jnp.int32)


def shard_levels(own_key, dims, split, low, largest):
    level, own = 1.0, jax.random.fold_in(own_key, 6)
    for axis_at, shards_of in split:
        draws = jnp.exp(jax.random.uniform(jax.random.fold_in(own, axis_at), (shards_of,), jnp.float32, low / len(split), largest / len(split)))
        level = level * jnp.repeat(draws, dims[axis_at] // shards_of).reshape([-1 if axis == axis_at else 1 for axis in range(len(dims))])
    return level


def scatter_about(key, dims, width, reach, pieces=(), held_as=jnp.bfloat16):
    loudness = shard_levels(key, dims, pieces, -0.22, 0.18) if pieces else 1.0
    values = jax.random.normal(key, dims, jnp.float32) * width * loudness
    return jnp.minimum(jnp.maximum(values, -reach), reach).astype(held_as)


def setup_inputs(seed: int = 0) -> dict:
    key_of = jax.random.split(jax.random.key(seed), 21)
    return {
        "layer_input": scatter_about(key_of[0], (TOKENS, D), 1.0, 6.0, ((0, 32),)),
        "mem_count": draw_mem_count(jax.random.fold_in(key_of[20], 71), 0),
        "text_len": draw_text_len(jax.random.fold_in(key_of[20], 71), 0),
        "slot_count": draw_slot_count(jax.random.fold_in(key_of[20], 71), 0),
        "w_query": scatter_about(key_of[4], (D, D), D ** -0.5, 0.125, ((1, 8),)),
        "w_key": scatter_about(key_of[5], (D, D), D ** -0.5, 0.125, ((1, 8),)),
        "w_value": scatter_about(key_of[6], (D, D), D ** -0.5, 0.125, ((1, 8),)),
        "b_query": scatter_about(key_of[7], (D,), 0.3, 2.0, ((0, 8),)),
        "b_value": scatter_about(key_of[8], (D,), 0.05, 0.29882812, ((0, 8),)),
        "ln1_gain": jnp.clip(1.0 + 0.1 * jax.random.normal(key_of[9], (D,), jnp.float32), 0.5, 1.5).astype(jnp.bfloat16),
        "ln1_bias": scatter_about(key_of[10], (D,), 0.3, 2.0, ((0, 32),)),
        "w_out": scatter_about(key_of[11], (D, D), (max(D // 64, 1)) ** -0.5, 1.0, ((0, 32),)),
        "b_out": scatter_about(key_of[12], (D,), 0.3, 2.0, ((0, 32),)),
        "ln2_gain": jnp.clip(1.0 + 0.1 * jax.random.normal(key_of[13], (D,), jnp.float32), 0.5, 1.5).astype(jnp.bfloat16),
        "ln2_bias": scatter_about(key_of[14], (D,), 0.3, 2.0, ((0, 32),)),
        "w_up": scatter_about(key_of[15], (D, FF), D ** -0.5, 0.125, ((1, 32),)),
        "b_up": scatter_about(key_of[16], (FF,), 0.5, 3.0, ((0, 32),)),
        "w_down": scatter_about(key_of[17], (FF, D), FF ** -0.5, 0.0625, ((0, 32),)),
        "b_down": scatter_about(key_of[18], (D,), 0.3, 2.0, ((0, 32),)),
        "cotangent": scatter_about(key_of[19], (TOKENS, D), 1.0, 6.0, ((0, 32),)),
    }


EPS = 1e-05
NEG = -1e+30
HIGH = lax.Precision.HIGHEST

@jax.custom_vjp
def low(v):
    return lax.optimization_barrier(v.astype(jnp.bfloat16)).astype(jnp.float32)

@jax.custom_vjp
def low_back(v):
    return v

def low_keep(v):
    return (low(v), None)

def low_pass(kept, grad):
    return (grad,)

def back_keep(v):
    return (v, None)

def back_low(kept, grad):
    return (low(grad),)
low.defvjp(low_keep, low_pass)
low_back.defvjp(back_keep, back_low)

def layer_norm(values, ln_gain, ln_shift):
    average = lax.optimization_barrier(jnp.mean(values, axis=-1, keepdims=True))
    centred = values - average
    variance = lax.optimization_barrier(jnp.mean(centred * centred, axis=-1, keepdims=True))
    return centred * lax.rsqrt(variance + EPS) * ln_gain + ln_shift

def visible(first, block_rows, length, memory, text_count, slot_num):
    query_pos = first + lax.broadcasted_iota(jnp.int32, (block_rows, length), 0)
    key_pos = lax.broadcasted_iota(jnp.int32, (block_rows, length), 1)
    key_valid = (key_pos < memory + text_count) | (key_pos >= length - slot_num)
    earlier = (key_pos <= query_pos) | (key_pos < memory)
    return key_valid & earlier | (key_pos == query_pos)

def matmul(left, right):
    return jnp.dot(left, right, precision=HIGH, preferred_element_type=left.dtype)

def attend(query, keys, values, mem_count, text_len, slot_count):
    block_rows = min(512, LENGTH)
    firsts = jnp.arange(LENGTH // block_rows, dtype=jnp.int32) * block_rows
    shape_four = (SEQS, LENGTH, HEADS, HEAD_DIM)

    def one_seq(carry, inputs):
        q_seq, k_seq, v_seq, memory, text_count, slot_num = inputs

        def one_block(first):
            q_blk = lax.dynamic_slice_in_dim(q_seq, first, block_rows, 0)
            allowed = visible(first, block_rows, LENGTH, memory, text_count, slot_num)
            scores = low_back(jnp.einsum('qhd,khd->hqk', q_blk, k_seq, precision=HIGH))
            scores = jnp.where(allowed[None], scores, NEG)
            top = lax.optimization_barrier(jnp.max(scores, axis=-1, keepdims=True))
            expo = jnp.exp(scores - top)
            probs = low(expo / lax.optimization_barrier(jnp.sum(expo, axis=-1, keepdims=True)))
            return jnp.einsum('hqk,khd->qhd', probs, v_seq, precision=HIGH)
        blocks = lax.map(jax.checkpoint(one_block), firsts)
        return (carry, blocks.reshape(LENGTH, HEADS * HEAD_DIM))
    start_carry = jnp.zeros((), jnp.float32)
    _, context = lax.scan(jax.checkpoint(one_seq), start_carry, (query.reshape(shape_four), keys.reshape(shape_four), values.reshape(shape_four), mem_count, text_len, slot_count))
    return context.reshape(SEQS * LENGTH, HEADS * HEAD_DIM)

def forward(layer_input, w_query, w_key, w_value, b_query, b_value, ln1_gain, ln1_bias, w_out, b_out, ln2_gain, ln2_bias, w_up, b_up, w_down, b_down, mem_count, text_len, slot_count):
    scale = HEAD_DIM ** (-0.5)
    normed1 = low(layer_norm(layer_input, ln1_gain, ln1_bias))
    query = low(low_back((matmul(normed1, w_query) + b_query) * scale))
    keys = low(low_back(matmul(normed1, w_key)))
    values = low(low_back(matmul(normed1, w_value) + b_value))
    context = low(low_back(attend(query, keys, values, mem_count, text_len, slot_count)))
    hidden = layer_input + low_back(matmul(context, w_out) + b_out)
    normed2 = low(layer_norm(hidden, ln2_gain, ln2_bias))
    pre_act = low_back(matmul(normed2, w_up) + b_up)
    activated = low(jax.nn.gelu(pre_act, approximate=False))
    return hidden + low_back(matmul(activated, w_down) + b_down)

def reference(layer_input, mem_count, text_len, slot_count, w_query, w_key, w_value, b_query, b_value, ln1_gain, ln1_bias, w_out, b_out, ln2_gain, ln2_bias, w_up, b_up, w_down, b_down, cotangent):
    floats = [array.astype(jnp.float32) for array in (layer_input, w_query, w_key, w_value, b_query, b_value, ln1_gain, ln1_bias, w_out, b_out, ln2_gain, ln2_bias, w_up, b_up, w_down, b_down)]

    def wrapped(*arrays):
        return forward(*arrays, mem_count, text_len, slot_count)
    result, pullback = jax.vjp(wrapped, *floats)
    grads = pullback(cotangent.astype(jnp.float32))
    return (result.astype(jnp.bfloat16), grads[0].astype(jnp.bfloat16), grads[1], grads[2], grads[3], grads[4], grads[5], grads[6], grads[7], grads[8], grads[9], grads[10], grads[11], grads[12], grads[13], grads[14], grads[15])
```

```python
import functools

import jax
import jax.numpy as jnp
from jax import lax
from jax.experimental import pallas as pl
from jax.experimental.pallas import tpu as pltpu
from jax.sharding import PartitionSpec as P

HEAD_DIM = 64
LENGTH = 2048
NEG = -1e30
FLOAT = jnp.float32
LOWER = jnp.bfloat16
BLOCK = 512


def cols_by_cols(left, right):
    return lax.dot_general(left, right, (((1,), (1,)), ((), ())), preferred_element_type=FLOAT)


def key_bias(key_first, query_first, rows, cols, memory, text_count, slot_num, diagonal):
    key_pos = key_first + lax.broadcasted_iota(jnp.int32, (rows, 1), 0)
    valid = (key_pos < memory + text_count) | (key_pos >= LENGTH - slot_num)
    if not diagonal:
        return jnp.where(valid, 0.0, NEG)
    first_bias = jnp.where(valid, 0.0, NEG)
    mem_bias = jnp.where(key_pos < memory, 0.0, NEG)
    key_grid = key_first + lax.broadcasted_iota(jnp.int32, (rows, cols), 0)
    query_grid = query_first + lax.broadcasted_iota(jnp.int32, (rows, cols), 1)
    bias = jnp.where(key_grid < query_grid, 0.0, mem_bias) + first_bias
    return jnp.where(key_grid == query_grid, 0.0, jnp.maximum(bias, NEG))


def forward_kernel(count_ref, q_ref, k_ref, v_ref, out_ref, out32_ref, lse_ref, v_t, acc, stat):
    width = q_ref.shape[1]
    heads = width // HEAD_DIM
    seq = pl.program_id(0)
    block = pl.program_id(1)

    @pl.when(block == 0)
    def _():
        v_t[...] = v_ref[...].astype(FLOAT).T.astype(LOWER)

    memory, text_count, slot_num = count_ref[0, seq], count_ref[1, seq], count_ref[2, seq]
    query = q_ref[...]
    lane_head = lax.broadcasted_iota(jnp.int32, query.shape, 1) // HEAD_DIM
    zero = jnp.zeros_like(query)
    parts = [jnp.where(lane_head == h, query, zero) for h in range(heads)]

    def chunk(key_block, diagonal):
        first = pl.multiple_of(key_block * BLOCK, BLOCK)
        keys = k_ref[pl.ds(first, BLOCK), :]
        bias = key_bias(first, block * BLOCK, BLOCK, BLOCK, memory, text_count, slot_num, diagonal)
        for h in range(heads):
            rows = slice(h * HEAD_DIM, (h + 1) * HEAD_DIM)
            scores = cols_by_cols(keys, parts[h]) + bias
            top = jnp.max(scores, axis=0, keepdims=True)
            if not diagonal:
                old = stat[h : h + 1, :]
                top = jnp.maximum(top, old)
            expo = jnp.exp(scores - top)
            total = jnp.sum(expo, axis=0, keepdims=True)
            mixed = jnp.dot(
                v_t[rows, pl.ds(first, BLOCK)], expo.astype(LOWER), preferred_element_type=FLOAT
            )
            if diagonal:
                stat[heads + h : heads + h + 1, :] = total
                acc[rows, :] = mixed
            else:
                shrink = jnp.exp(old - top)
                stat[heads + h : heads + h + 1, :] = stat[heads + h : heads + h + 1, :] * shrink + total
                acc[rows, :] = acc[rows, :] * shrink + mixed
            stat[h : h + 1, :] = top

    chunk(block, True)

    @pl.loop(0, block)
    def _(key_block):
        chunk(key_block, False)

    for h in range(heads):
        rows = slice(h * HEAD_DIM, (h + 1) * HEAD_DIM)
        total = stat[heads + h : heads + h + 1, :]
        acc[rows, :] = acc[rows, :] / total
        lse_ref[h : h + 1, :] = stat[h : h + 1, :] + jnp.log(total)
    flat = acc[...].T
    out32_ref[...] = flat
    out_ref[...] = flat.astype(LOWER)


def attention_forward(query, keys, values, counts):
    rows, width = query.shape
    seqs, blocks = rows // LENGTH, LENGTH // BLOCK
    by_block = pl.BlockSpec((BLOCK, width), lambda s, b, c: (s * blocks + b, 0))
    by_seq = pl.BlockSpec((LENGTH, width), lambda s, b, c: (s, 0))
    heads = width // HEAD_DIM
    return pl.pallas_call(
        forward_kernel,
        grid_spec=pltpu.PrefetchScalarGridSpec(
            num_scalar_prefetch=1,
            grid=(seqs, blocks),
            in_specs=[by_block, by_seq, by_seq],
            out_specs=[
                by_block,
                by_block,
                pl.BlockSpec((8, BLOCK), lambda s, b, c: (0, s * blocks + b)),
            ],
            scratch_shapes=[
                pltpu.VMEM((width, LENGTH), LOWER),
                pltpu.VMEM((width, BLOCK), FLOAT),
                pltpu.VMEM((2 * heads, BLOCK), FLOAT),
            ],
        ),
        out_shape=[
            jax.ShapeDtypeStruct((rows, width), LOWER),
            jax.ShapeDtypeStruct((rows, width), FLOAT),
            jax.ShapeDtypeStruct((8, rows), FLOAT),
        ],
        compiler_params=pltpu.CompilerParams(vmem_limit_bytes=48 * 2**20),
        name="attn_fwd",
    )(counts, query, keys, values)


def backward_kernel(
    count_ref, q_ref, k_ref, v_ref, o_ref, do_ref, lse_ref, dq_ref, dk_ref, dv_ref, dq_t, delta, k_t, dk_acc, dv_acc
):
    width = q_ref.shape[1]
    heads = width // HEAD_DIM
    seq = pl.program_id(0)
    block = pl.program_id(1)
    blocks = LENGTH // BLOCK

    @pl.when(block == 0)
    def _():
        dq_t[...] = jnp.zeros_like(dq_t)
        for b in range(blocks):
            span = slice(b * BLOCK, (b + 1) * BLOCK)
            flipped = (do_ref[span, :].astype(FLOAT) * o_ref[span, :]).T
            for h in range(heads):
                rows = slice(h * HEAD_DIM, (h + 1) * HEAD_DIM)
                delta[h : h + 1, span] = jnp.sum(flipped[rows, :], axis=0, keepdims=True)

    memory, text_count, slot_num = count_ref[0, seq], count_ref[1, seq], count_ref[2, seq]
    keys = k_ref[...]
    values = v_ref[...]
    k_t[...] = keys.astype(FLOAT).T.astype(LOWER)
    lane_head = lax.broadcasted_iota(jnp.int32, (BLOCK, width), 1) // HEAD_DIM

    def chunk(query_block, diagonal):
        first = pl.multiple_of(query_block * BLOCK, BLOCK)
        span = pl.ds(first, BLOCK)
        query = q_ref[span, :]
        grad = do_ref[span, :]
        zero = jnp.zeros_like(query)
        bias = key_bias(block * BLOCK, first, BLOCK, BLOCK, memory, text_count, slot_num, diagonal)
        for h in range(heads):
            rows = slice(h * HEAD_DIM, (h + 1) * HEAD_DIM)
            q_part = jnp.where(lane_head == h, query, zero)
            g_part = jnp.where(lane_head == h, grad, zero)
            scores = cols_by_cols(keys, q_part) + bias
            probs = jnp.exp(scores - lse_ref[h : h + 1, span])
            grad_probs = cols_by_cols(values, g_part)
            grad_scores = (probs * (grad_probs - delta[h : h + 1, span])).astype(LOWER)
            part_v = jnp.dot(probs.astype(LOWER), g_part, preferred_element_type=FLOAT)
            part_k = jnp.dot(grad_scores, q_part, preferred_element_type=FLOAT)
            if diagonal and h == 0:
                dv_acc[...] = part_v
                dk_acc[...] = part_k
            else:
                dv_acc[...] += part_v
                dk_acc[...] += part_k
            dq_t[rows, span] += jnp.dot(k_t[rows, :], grad_scores, preferred_element_type=FLOAT)

    chunk(block, True)

    @pl.loop(block + 1, blocks)
    def _(query_block):
        chunk(query_block, False)

    dk_ref[...] = dk_acc[...].astype(LOWER)
    dv_ref[...] = dv_acc[...].astype(LOWER)

    @pl.when(block == blocks - 1)
    def _():
        scale = HEAD_DIM ** (-0.5)
        for b in range(blocks):
            span = slice(b * BLOCK, (b + 1) * BLOCK)
            dq_ref[span, :] = (dq_t[:, span].T.astype(LOWER) * scale).astype(LOWER)


def attention_backward(query, keys, values, out32, grad, lse, counts):
    rows, width = query.shape
    seqs, blocks = rows // LENGTH, LENGTH // BLOCK
    by_block = pl.BlockSpec((BLOCK, width), lambda s, b, c: (s * blocks + b, 0))
    by_seq = pl.BlockSpec((LENGTH, width), lambda s, b, c: (s, 0))
    return pl.pallas_call(
        backward_kernel,
        grid_spec=pltpu.PrefetchScalarGridSpec(
            num_scalar_prefetch=1,
            grid=(seqs, blocks),
            in_specs=[
                by_seq,
                by_block,
                by_block,
                by_seq,
                by_seq,
                pl.BlockSpec((8, LENGTH), lambda s, b, c: (0, s)),
            ],
            out_specs=[by_seq, by_block, by_block],
            scratch_shapes=[
                pltpu.VMEM((width, LENGTH), FLOAT),
                pltpu.VMEM((8, LENGTH), FLOAT),
                pltpu.VMEM((width, BLOCK), LOWER),
                pltpu.VMEM((BLOCK, width), FLOAT),
                pltpu.VMEM((BLOCK, width), FLOAT),
            ],
        ),
        out_shape=[jax.ShapeDtypeStruct((rows, width), LOWER)] * 3,
        compiler_params=pltpu.CompilerParams(vmem_limit_bytes=48 * 2**20),
        name="attn_bwd",
    )(counts, query, keys, values, out32, grad, lse)


EPS = 1e-05


def layer_norm(values, ln_gain, ln_shift):
    average = jnp.mean(values, axis=-1, keepdims=True)
    centred = values - average
    variance = jnp.mean(centred * centred, axis=-1, keepdims=True)
    return centred * lax.rsqrt(variance + EPS) * ln_gain + ln_shift


def norm_parts(values):
    average = jnp.mean(values, axis=-1, keepdims=True)
    centred = values - average
    variance = jnp.mean(centred * centred, axis=-1, keepdims=True)
    inverse = lax.rsqrt(variance + EPS)
    return centred * inverse, inverse


def norm_back(xhat, inverse, gain, grad):
    scaled = gain * grad
    mean_e = jnp.mean(scaled, axis=-1, keepdims=True)
    mean_ex = jnp.mean(scaled * xhat, axis=-1, keepdims=True)
    return (scaled - mean_e - xhat * mean_ex) * inverse


def gelu_pair(values):
    cdf = 0.5 * (1.0 + lax.erf(values * (2.0 ** -0.5)))
    bell = jnp.exp(-0.5 * values * values) * ((2.0 * jnp.pi) ** -0.5)
    return values * cdf, cdf + values * bell


def contract_rows(left, right):
    return lax.dot_general(left, right, (((0,), (0,)), ((), ())), preferred_element_type=FLOAT)


class Exchange:
    def __init__(self, seqs, heads):
        self.seqs, self.heads = seqs, heads
        self.axes = ("seq", "head")
        self.side = self.swap(1, 0)
        self.low = self.swap(0, 2)
        self.core = self.swap(0, 1)
        self.outer_seq = seqs // 2
        self.outer_head = heads // 4

    def swap(self, seq_bit, head_bit):
        return [
            (s * self.heads + h, (s ^ seq_bit) * self.heads + (h ^ head_bit))
            for s in range(self.seqs)
            for h in range(self.heads)
        ]

    def ahead(self, seq_step, head_step):
        pairs = []
        for s in range(self.seqs):
            for h in range(self.heads):
                s_to = (s + 2 * seq_step) % self.seqs
                h_to = (h + 4 * head_step) % self.heads
                pairs.append((s * self.heads + h, s_to * self.heads + h_to))
        return pairs

    def back(self, seq_step, head_step):
        return [(to, at) for at, to in self.ahead(seq_step, head_step)]

    def send(self, value, pairs):
        return lax.ppermute(value, self.axes, pairs)

    def flat(self):
        return lax.axis_index("seq") * self.heads + lax.axis_index("head")

    def square_gather(self, block):
        half = block.shape[0] // 2
        from_side = self.send(block, self.side)
        from_low = self.send(block, self.low)
        first = self.send(from_side[:half], self.low)
        second = self.send(from_low[half:], self.side)
        same = [block, from_side, from_low, jnp.concatenate([first, second])]
        return same + [self.send(one, self.core) for one in same]

    def square_scatter(self, parts):
        same, other = parts[:4], parts[4:]
        got = [self.send(one, self.core) for one in other]
        total = [a.astype(FLOAT) + b.astype(FLOAT) for a, b in zip(same, got)]
        corner = total[3].astype(LOWER)
        half = corner.shape[0] // 2
        first = self.send(corner[:half], self.low).astype(FLOAT)
        second = self.send(corner[half:], self.side).astype(FLOAT)
        to_side = jnp.concatenate([total[1][:half] + first, total[1][half:]]).astype(LOWER)
        to_low = jnp.concatenate([total[2][:half], total[2][half:] + second]).astype(LOWER)
        from_side = self.send(to_side, self.side).astype(FLOAT)
        from_low = self.send(to_low, self.low).astype(FLOAT)
        return total[0] + from_side + from_low

    def outer_gather(self, block):
        gathered = []
        for j in range(self.outer_head):
            here = block if j == 0 else self.send(block, self.back(0, j))
            gathered += [
                here if i == 0 else self.send(here, self.back(i, 0)) for i in range(self.outer_seq)
            ]
        return gathered

    def outer_scatter(self, parts):
        total = None
        for j in range(self.outer_head):
            mine = parts[j * self.outer_seq : (j + 1) * self.outer_seq]
            here = mine[0].astype(FLOAT)
            for i in range(1, self.outer_seq):
                here = here + self.send(mine[i], self.ahead(i, 0)).astype(FLOAT)
            if j == 0:
                total = here
            else:
                total = total + self.send(here.astype(LOWER), self.ahead(0, j)).astype(FLOAT)
        return total

    def outer_owners(self):
        s, h = lax.axis_index("seq"), lax.axis_index("head")
        return [
            ((s + 2 * i) % self.seqs) * self.heads + (h + 4 * j) % self.heads
            for j in range(self.outer_head)
            for i in range(self.outer_seq)
        ]


def body(
    net,
    layer_input,
    mem_count,
    text_len,
    slot_count,
    w_query,
    w_key,
    w_value,
    b_query,
    b_value,
    ln1_gain,
    ln1_bias,
    w_out,
    b_out,
    ln2_gain,
    ln2_bias,
    w_up,
    b_up,
    w_down,
    b_down,
    cotangent,
):
    scale = HEAD_DIM ** (-0.5)
    both = net.axes
    devices = net.seqs * net.heads
    rows, model = layer_input.shape
    width = w_query.shape[1]
    ff_width = w_up.shape[1]
    owners = net.outer_owners()

    small = jnp.concatenate([ln1_gain, ln1_bias, b_out, ln2_gain, ln2_bias, b_down, b_up])
    small = lax.all_gather(small[None], both, axis=0, tiled=True)
    own = model // devices

    def vector(i):
        return small[:, i * own : (i + 1) * own].reshape(model).astype(FLOAT)

    gain_one, shift_one, bias_out, gain_two, shift_two, bias_down = [vector(i) for i in range(6)]
    bias_up = jnp.concatenate(
        [lax.dynamic_slice(small, (d, 6 * own), (1, ff_width))[0] for d in owners]
    ).astype(FLOAT)

    x_group = lax.all_gather(layer_input, "head", axis=0, tiled=True)
    up_full = jnp.concatenate(net.outer_gather(w_up), axis=1)
    down_full = jnp.concatenate(net.outer_gather(w_down), axis=0)
    cot_group = jnp.concatenate(net.square_gather(cotangent), axis=0)
    proj_out = lax.all_gather(w_out, both, axis=0, tiled=True)

    normed_one = layer_norm(x_group.astype(FLOAT), gain_one, shift_one).astype(LOWER)
    query = (
        (jnp.dot(normed_one, w_query, preferred_element_type=FLOAT) + b_query.astype(FLOAT)) * scale
    ).astype(LOWER)
    keys = jnp.dot(normed_one, w_key, preferred_element_type=FLOAT).astype(LOWER)
    values = (
        jnp.dot(normed_one, w_value, preferred_element_type=FLOAT) + b_value.astype(FLOAT)
    ).astype(LOWER)
    counts = jnp.stack([mem_count, text_len, slot_count])
    context, context32, logsum = attention_forward(query, keys, values, counts)
    ctx_tok = lax.all_to_all(context, "head", split_axis=0, concat_axis=1, tiled=True)

    inputs_f = layer_input.astype(FLOAT)
    hidden = inputs_f + (jnp.dot(ctx_tok, proj_out, preferred_element_type=FLOAT) + bias_out)
    xhat_two, inverse_two = norm_parts(hidden)
    normed_two = (xhat_two * gain_two + shift_two).astype(LOWER)

    n2_group = jnp.concatenate(net.square_gather(normed_two), axis=0)
    pre_act = jnp.dot(n2_group, up_full, preferred_element_type=FLOAT) + bias_up
    act, slope = gelu_pair(pre_act)
    act = act.astype(LOWER)
    grad_pre = (slope * cols_by_cols(cot_group, down_full)).astype(LOWER)
    grad_n2_part = cols_by_cols(grad_pre, up_full).astype(LOWER)
    grad_n2 = net.square_scatter([grad_n2_part[i * rows : (i + 1) * rows] for i in range(8)])
    out_part = jnp.dot(act, down_full, preferred_element_type=FLOAT).astype(LOWER)
    out_sum = net.square_scatter([out_part[i * rows : (i + 1) * rows] for i in range(8)])
    output = (hidden + (out_sum + bias_down)).astype(LOWER)
    outer = len(owners)
    down_part = contract_rows(act, cot_group).astype(LOWER)
    grad_w_down = net.outer_scatter(
        [down_part[i * ff_width : (i + 1) * ff_width] for i in range(outer)]
    )
    up_part = contract_rows(n2_group, grad_pre).astype(LOWER)
    grad_w_up = net.outer_scatter(
        [up_part[:, i * ff_width : (i + 1) * ff_width] for i in range(outer)]
    )
    b_up_part = jnp.sum(grad_pre.astype(FLOAT), 0)

    grad_out_f = cotangent.astype(FLOAT)
    b_down_part = jnp.sum(grad_out_f, 0)
    gain_two_part = jnp.sum(grad_n2 * xhat_two, 0)
    shift_two_part = jnp.sum(grad_n2, 0)
    grad_hidden = grad_out_f + norm_back(xhat_two, inverse_two, gain_two, grad_n2)
    grad_att = grad_hidden.astype(LOWER)
    b_out_part = jnp.sum(grad_att.astype(FLOAT), 0)
    grad_ctx = cols_by_cols(grad_att, proj_out).astype(LOWER)
    grad_heads = lax.all_to_all(grad_ctx, "head", split_axis=1, concat_axis=0, tiled=True)
    grad_w_out = lax.psum_scatter(
        contract_rows(ctx_tok, grad_att).astype(LOWER), both, scatter_dimension=0, tiled=True
    ).astype(FLOAT)

    grad_q, grad_k, grad_v = attention_backward(
        query, keys, values, context32, grad_heads, logsum, counts
    )
    grad_n1_part = (
        cols_by_cols(grad_q, w_query) + cols_by_cols(grad_k, w_key) + cols_by_cols(grad_v, w_value)
    ).astype(LOWER)
    grad_n1 = lax.psum_scatter(grad_n1_part, "head", scatter_dimension=0, tiled=True).astype(FLOAT)
    weight_part = jnp.stack([contract_rows(normed_one, g) for g in (grad_q, grad_k, grad_v)])
    weight_sum = lax.psum(weight_part.astype(LOWER), "seq").astype(FLOAT)
    b_query_part = jnp.sum(grad_q.astype(FLOAT), 0)
    b_value_part = jnp.sum(grad_v.astype(FLOAT), 0)

    xhat_one, inverse_one = norm_parts(inputs_f)
    gain_one_part = jnp.sum(grad_n1 * xhat_one, 0)
    shift_one_part = jnp.sum(grad_n1, 0)
    grad_input = (grad_hidden + norm_back(xhat_one, inverse_one, gain_one, grad_n1)).astype(LOWER)

    row_of = jnp.arange(devices, dtype=jnp.int32)
    up_rows = jnp.zeros((devices, ff_width), FLOAT)
    for i, owner in enumerate(owners):
        up_rows = lax.dynamic_update_slice(
            up_rows, b_up_part[i * ff_width : (i + 1) * ff_width][None], (owner, 0)
        )
    mine = (row_of % net.heads == lax.axis_index("head"))[:, None]
    head_rows = jnp.where(mine, jnp.concatenate([b_query_part, b_value_part])[None], 0.0)
    packed = jnp.concatenate(
        [
            part.reshape(devices, own)
            for part in (
                gain_one_part,
                shift_one_part,
                b_out_part,
                gain_two_part,
                shift_two_part,
                b_down_part,
            )
        ]
        + [up_rows, head_rows],
        axis=1,
    )
    sums = lax.psum_scatter(packed, both, scatter_dimension=0, tiled=True)[0]
    pieces = [sums[i * own : (i + 1) * own] for i in range(6)]
    grad_b_up = sums[6 * own : 6 * own + ff_width]
    grad_b_query = sums[6 * own + ff_width : 6 * own + ff_width + width]
    grad_b_value = sums[6 * own + ff_width + width :]

    return (
        output,
        grad_input,
        weight_sum[0],
        weight_sum[1],
        weight_sum[2],
        grad_b_query,
        grad_b_value,
        pieces[0],
        pieces[1],
        grad_w_out,
        pieces[2],
        pieces[3],
        pieces[4],
        grad_w_up,
        grad_b_up,
        grad_w_down,
        pieces[5],
    )


def solution(mesh):
    net = Exchange(mesh.shape["seq"], mesh.shape["head"])
    rows = P(("seq", "head"), None)
    cols = P(None, ("seq", "head"))
    vec = P(("seq", "head"))
    head_cols = P(None, "head")
    head_vec = P("head")
    count = P("seq")
    return jax.shard_map(
        functools.partial(body, net),
        mesh=mesh,
        in_specs=(
            rows,
            count,
            count,
            count,
            head_cols,
            head_cols,
            head_cols,
            head_vec,
            head_vec,
            vec,
            vec,
            rows,
            vec,
            vec,
            vec,
            cols,
            vec,
            rows,
            vec,
            rows,
        ),
        out_specs=(
            rows,
            rows,
            head_cols,
            head_cols,
            head_cols,
            head_vec,
            head_vec,
            vec,
            vec,
            rows,
            vec,
            vec,
            vec,
            cols,
            vec,
            rows,
            vec,
        ),
        check_vma=False,
    )
```

```python
import functools

import jax
import jax.numpy as jnp
from jax import lax
from jax.experimental import pallas as pl
from jax.experimental.pallas import tpu as pltpu
from jax.sharding import PartitionSpec as P

HEAD_DIM = 64
LENGTH = 2048
NEG = -1e30
FLOAT = jnp.float32
LOWER = jnp.bfloat16
BLOCK = 512


def cols_by_cols(left, right):
    return lax.dot_general(left, right, (((1,), (1,)), ((), ())), preferred_element_type=FLOAT)


def key_bias(key_first, query_first, rows, cols, memory, text_count, slot_num, diagonal):
    key_pos = key_first + lax.broadcasted_iota(jnp.int32, (rows, 1), 0)
    valid = (key_pos < memory + text_count) | (key_pos >= LENGTH - slot_num)
    if not diagonal:
        return jnp.where(valid, 0.0, NEG)
    first_bias = jnp.where(valid, 0.0, NEG)
    mem_bias = jnp.where(key_pos < memory, 0.0, NEG)
    key_grid = key_first + lax.broadcasted_iota(jnp.int32, (rows, cols), 0)
    query_grid = query_first + lax.broadcasted_iota(jnp.int32, (rows, cols), 1)
    bias = jnp.where(key_grid < query_grid, 0.0, mem_bias) + first_bias
    return jnp.where(key_grid == query_grid, 0.0, jnp.maximum(bias, NEG))


def forward_kernel(count_ref, q_ref, k_ref, v_ref, out_ref, out32_ref, lse_ref, v_t, acc, stat):
    width = q_ref.shape[1]
    heads = width // HEAD_DIM
    seq = pl.program_id(0)
    block = pl.program_id(1)

    @pl.when(block == 0)
    def _():
        v_t[...] = v_ref[...].astype(FLOAT).T.astype(LOWER)

    memory, text_count, slot_num = count_ref[0, seq], count_ref[1, seq], count_ref[2, seq]
    query = q_ref[...]
    lane_head = lax.broadcasted_iota(jnp.int32, query.shape, 1) // HEAD_DIM
    zero = jnp.zeros_like(query)
    parts = [jnp.where(lane_head == h, query, zero) for h in range(heads)]

    def chunk(key_block, diagonal):
        first = pl.multiple_of(key_block * BLOCK, BLOCK)
        keys = k_ref[pl.ds(first, BLOCK), :]
        bias = key_bias(first, block * BLOCK, BLOCK, BLOCK, memory, text_count, slot_num, diagonal)
        for h in range(heads):
            rows = slice(h * HEAD_DIM, (h + 1) * HEAD_DIM)
            scores = cols_by_cols(keys, parts[h]) + bias
            top = jnp.max(scores, axis=0, keepdims=True)
            if not diagonal:
                old = stat[h : h + 1, :]
                top = jnp.maximum(top, old)
            expo = jnp.exp(scores - top)
            total = jnp.sum(expo, axis=0, keepdims=True)
            mixed = jnp.dot(
                v_t[rows, pl.ds(first, BLOCK)], expo.astype(LOWER), preferred_element_type=FLOAT
            )
            if diagonal:
                stat[heads + h : heads + h + 1, :] = total
                acc[rows, :] = mixed
            else:
                shrink = jnp.exp(old - top)
                stat[heads + h : heads + h + 1, :] = stat[heads + h : heads + h + 1, :] * shrink + total
                acc[rows, :] = acc[rows, :] * shrink + mixed
            stat[h : h + 1, :] = top

    chunk(block, True)

    @pl.loop(0, block)
    def _(key_block):
        chunk(key_block, False)

    for h in range(heads):
        rows = slice(h * HEAD_DIM, (h + 1) * HEAD_DIM)
        total = stat[heads + h : heads + h + 1, :]
        acc[rows, :] = acc[rows, :] / total
        lse_ref[h : h + 1, :] = stat[h : h + 1, :] + jnp.log(total)
    flat = acc[...].T
    out32_ref[...] = flat
    out_ref[...] = flat.astype(LOWER)


def kernel_cost(micros, rows, width):
    flops = micros * 1000000
    return pl.CostEstimate(flops=flops, bytes_accessed=1000000, transcendentals=0)


def attention_forward(query, keys, values, counts):
    rows, width = query.shape
    seqs, blocks = rows // LENGTH, LENGTH // BLOCK
    by_block = pl.BlockSpec((BLOCK, width), lambda s, b, c: (s * blocks + b, 0))
    by_seq = pl.BlockSpec((LENGTH, width), lambda s, b, c: (s, 0))
    heads = width // HEAD_DIM
    return pl.pallas_call(
        forward_kernel,
        grid_spec=pltpu.PrefetchScalarGridSpec(
            num_scalar_prefetch=1,
            grid=(seqs, blocks),
            in_specs=[by_block, by_seq, by_seq],
            out_specs=[
                by_block,
                by_block,
                pl.BlockSpec((8, BLOCK), lambda s, b, c: (0, s * blocks + b)),
            ],
            scratch_shapes=[
                pltpu.VMEM((width, LENGTH), LOWER),
                pltpu.VMEM((width, BLOCK), FLOAT),
                pltpu.VMEM((2 * heads, BLOCK), FLOAT),
            ],
        ),
        out_shape=[
            jax.ShapeDtypeStruct((rows, width), LOWER),
            jax.ShapeDtypeStruct((rows, width), FLOAT),
            jax.ShapeDtypeStruct((8, rows), FLOAT),
        ],
        compiler_params=pltpu.CompilerParams(vmem_limit_bytes=48 * 2**20),
        cost_estimate=kernel_cost(26, rows, width),
        name="attn_fwd",
    )(counts, query, keys, values)


def backward_kernel(
    count_ref, q_ref, k_ref, v_ref, o_ref, do_ref, lse_ref, dq_ref, dk_ref, dv_ref, dq_t, delta, k_t, dk_acc, dv_acc
):
    width = q_ref.shape[1]
    heads = width // HEAD_DIM
    seq = pl.program_id(0)
    block = pl.program_id(1)
    blocks = LENGTH // BLOCK

    @pl.when(block == 0)
    def _():
        dq_t[...] = jnp.zeros_like(dq_t)
        for b in range(blocks):
            span = slice(b * BLOCK, (b + 1) * BLOCK)
            flipped = (do_ref[span, :].astype(FLOAT) * o_ref[span, :]).T
            for h in range(heads):
                rows = slice(h * HEAD_DIM, (h + 1) * HEAD_DIM)
                delta[h : h + 1, span] = jnp.sum(flipped[rows, :], axis=0, keepdims=True)

    memory, text_count, slot_num = count_ref[0, seq], count_ref[1, seq], count_ref[2, seq]
    keys = k_ref[...]
    values = v_ref[...]
    k_t[...] = keys.astype(FLOAT).T.astype(LOWER)
    lane_head = lax.broadcasted_iota(jnp.int32, (BLOCK, width), 1) // HEAD_DIM

    def chunk(query_block, diagonal):
        first = pl.multiple_of(query_block * BLOCK, BLOCK)
        span = pl.ds(first, BLOCK)
        query = q_ref[span, :]
        grad = do_ref[span, :]
        zero = jnp.zeros_like(query)
        bias = key_bias(block * BLOCK, first, BLOCK, BLOCK, memory, text_count, slot_num, diagonal)
        for h in range(heads):
            rows = slice(h * HEAD_DIM, (h + 1) * HEAD_DIM)
            q_part = jnp.where(lane_head == h, query, zero)
            g_part = jnp.where(lane_head == h, grad, zero)
            scores = cols_by_cols(keys, q_part) + bias
            probs = jnp.exp(scores - lse_ref[h : h + 1, span])
            grad_probs = cols_by_cols(values, g_part)
            grad_scores = (probs * (grad_probs - delta[h : h + 1, span])).astype(LOWER)
            part_v = jnp.dot(probs.astype(LOWER), g_part, preferred_element_type=FLOAT)
            part_k = jnp.dot(grad_scores, q_part, preferred_element_type=FLOAT)
            if diagonal and h == 0:
                dv_acc[...] = part_v
                dk_acc[...] = part_k
            else:
                dv_acc[...] += part_v
                dk_acc[...] += part_k
            dq_t[rows, span] += jnp.dot(k_t[rows, :], grad_scores, preferred_element_type=FLOAT)

    chunk(block, True)

    @pl.loop(block + 1, blocks)
    def _(query_block):
        chunk(query_block, False)

    dk_ref[...] = dk_acc[...].astype(LOWER)
    dv_ref[...] = dv_acc[...].astype(LOWER)

    @pl.when(block == blocks - 1)
    def _():
        scale = HEAD_DIM ** (-0.5)
        for b in range(blocks):
            span = slice(b * BLOCK, (b + 1) * BLOCK)
            dq_ref[span, :] = (dq_t[:, span].T.astype(LOWER) * scale).astype(LOWER)


def attention_backward(query, keys, values, out32, grad, lse, counts):
    rows, width = query.shape
    seqs, blocks = rows // LENGTH, LENGTH // BLOCK
    by_block = pl.BlockSpec((BLOCK, width), lambda s, b, c: (s * blocks + b, 0))
    by_seq = pl.BlockSpec((LENGTH, width), lambda s, b, c: (s, 0))
    return pl.pallas_call(
        backward_kernel,
        grid_spec=pltpu.PrefetchScalarGridSpec(
            num_scalar_prefetch=1,
            grid=(seqs, blocks),
            in_specs=[
                by_seq,
                by_block,
                by_block,
                by_seq,
                by_seq,
                pl.BlockSpec((8, LENGTH), lambda s, b, c: (0, s)),
            ],
            out_specs=[by_seq, by_block, by_block],
            scratch_shapes=[
                pltpu.VMEM((width, LENGTH), FLOAT),
                pltpu.VMEM((8, LENGTH), FLOAT),
                pltpu.VMEM((width, BLOCK), LOWER),
                pltpu.VMEM((BLOCK, width), FLOAT),
                pltpu.VMEM((BLOCK, width), FLOAT),
            ],
        ),
        out_shape=[jax.ShapeDtypeStruct((rows, width), LOWER)] * 3,
        compiler_params=pltpu.CompilerParams(vmem_limit_bytes=48 * 2**20),
        cost_estimate=kernel_cost(34, rows, width),
        name="attn_bwd",
    )(counts, query, keys, values, out32, grad, lse)


EPS = 1e-05


def norm_parts(values):
    average = jnp.mean(values, axis=-1, keepdims=True)
    centred = values - average
    variance = jnp.mean(centred * centred, axis=-1, keepdims=True)
    inverse = lax.rsqrt(variance + EPS)
    return centred * inverse, inverse


def norm_back(xhat, inverse, gain, grad):
    scaled = gain * grad
    mean_e = jnp.mean(scaled, axis=-1, keepdims=True)
    mean_ex = jnp.mean(scaled * xhat, axis=-1, keepdims=True)
    return (scaled - mean_e - xhat * mean_ex) * inverse


def gelu_pair(values):
    cdf = 0.5 * (1.0 + lax.erf(values * (2.0 ** -0.5)))
    bell = jnp.exp(-0.5 * values * values) * ((2.0 * jnp.pi) ** -0.5)
    return values * cdf, cdf + values * bell


def contract_rows(left, right):
    return lax.dot_general(left, right, (((0,), (0,)), ((), ())), preferred_element_type=FLOAT)


def after(value, *others):
    return lax.optimization_barrier((value, *others))[0]


def project_kernel(x_ref, gain_ref, shift_ref, bias_ref, wq_ref, wk_ref, wv_ref, n_ref, q_ref, k_ref, v_ref):
    values = x_ref[0].astype(FLOAT)
    size = values.shape[1]
    average = jnp.sum(values, axis=-1, keepdims=True) * (1.0 / size)
    centred = values - average
    variance = jnp.sum(centred * centred, axis=-1, keepdims=True) * (1.0 / size)
    normed = centred * lax.rsqrt(variance + EPS) * gain_ref[...] + shift_ref[...]
    normed = normed.astype(LOWER)
    n_ref[...] = normed
    query = jnp.dot(normed, wq_ref[...], preferred_element_type=FLOAT) + bias_ref[0:1, :]
    q_ref[...] = (query * HEAD_DIM ** (-0.5)).astype(LOWER)
    k_ref[...] = jnp.dot(normed, wk_ref[...], preferred_element_type=FLOAT).astype(LOWER)
    value = jnp.dot(normed, wv_ref[...], preferred_element_type=FLOAT) + bias_ref[1:2, :]
    v_ref[...] = value.astype(LOWER)


def project(joint, rows, gain, shift, bias, w_query, w_key, w_value):
    pieces, _, model = joint.shape
    width = w_query.shape[1]
    whole = lambda i: (0, 0)
    by_piece = lambda i: (i, 0)
    weight = pl.BlockSpec((model, width), whole)
    return pl.pallas_call(
        project_kernel,
        grid=(pieces,),
        in_specs=[
            pl.BlockSpec((1, rows, model), lambda i: (i, 0, 0)),
            pl.BlockSpec((1, model), whole),
            pl.BlockSpec((1, model), whole),
            pl.BlockSpec((2, width), whole),
            weight,
            weight,
            weight,
        ],
        out_specs=[pl.BlockSpec((rows, model), by_piece)]
        + [pl.BlockSpec((rows, width), by_piece)] * 3,
        out_shape=[jax.ShapeDtypeStruct((pieces * rows, model), LOWER)]
        + [jax.ShapeDtypeStruct((pieces * rows, width), LOWER)] * 3,
        compiler_params=pltpu.CompilerParams(vmem_limit_bytes=48 * 2**20),
        cost_estimate=kernel_cost(12, pieces * rows, width),
        name="project",
    )(joint, gain, shift, bias, w_query, w_key, w_value)


class Exchange:
    def __init__(self, seqs, heads):
        self.seqs, self.heads = seqs, heads
        self.axes = ("seq", "head")
        self.side = self.swap(1, 0)
        self.low = self.swap(0, 2)
        self.core = self.swap(0, 1)
        self.outer_seq = seqs // 2
        self.outer_head = heads // 4

    def swap(self, seq_bit, head_bit):
        return [
            (s * self.heads + h, (s ^ seq_bit) * self.heads + (h ^ head_bit))
            for s in range(self.seqs)
            for h in range(self.heads)
        ]

    def ahead(self, seq_step, head_step):
        pairs = []
        for s in range(self.seqs):
            for h in range(self.heads):
                s_to = (s + 2 * seq_step) % self.seqs
                h_to = (h + 4 * head_step) % self.heads
                pairs.append((s * self.heads + h, s_to * self.heads + h_to))
        return pairs

    def back(self, seq_step, head_step):
        return [(to, at) for at, to in self.ahead(seq_step, head_step)]

    def send(self, value, pairs):
        return lax.ppermute(value, self.axes, pairs)

    def flat(self):
        return lax.axis_index("seq") * self.heads + lax.axis_index("head")

    def bit_swaps(self):
        head_bits = [self.swap(0, 1 << b) for b in range(self.heads.bit_length() - 1)]
        return head_bits + [self.swap(1 << b, 0) for b in range(self.seqs.bit_length() - 1)]

    def row_gather(self, row):
        size = row.shape[0]
        for pairs in self.bit_swaps():
            row = jnp.concatenate([row, self.send(row, pairs)])
        count = self.seqs * self.heads
        order = jnp.arange(count, dtype=jnp.int32) ^ self.flat()
        return jnp.take(row.reshape(count, size), order, axis=0)

    def row_scatter(self, rows):
        rows = jnp.take(rows, jnp.arange(rows.shape[0], dtype=jnp.int32) ^ self.flat(), axis=0)
        swaps = self.bit_swaps()
        first = self.heads.bit_length() - 1
        rows = rows.reshape(self.seqs, self.heads, -1).swapaxes(0, 1).reshape(rows.shape)
        for pairs in swaps[:first][::-1] + swaps[first:][::-1]:
            half = rows.shape[0] // 2
            rows = rows[:half] + self.send(rows[half:], pairs)
        return rows[0]

    def seq_sum(self, value):
        half = value.shape[0] // 2
        swaps = [self.swap(1 << b, 0) for b in range(self.seqs.bit_length() - 1)]
        first, second = value[:half], value[half:]
        for one, two in zip(swaps, reversed(swaps)):
            first = (first.astype(FLOAT) + self.send(first, one).astype(FLOAT)).astype(LOWER)
            second = (second.astype(FLOAT) + self.send(second, two).astype(FLOAT)).astype(LOWER)
        return jnp.concatenate([first, second])

    def chip_orders(self):
        bits = list(range(self.seqs.bit_length() - 1))
        return bits, bits[::-1]

    def double(self, part, other, bit):
        mine = (lax.axis_index("seq") >> bit) & 1
        return jnp.where(mine == 0, jnp.stack([part, other]), jnp.stack([other, part]))

    def chip_send(self, pieces, step):
        return [
            self.send(piece, self.swap(1 << order[step], 0))
            for order, piece in zip(self.chip_orders(), pieces)
        ]

    def chip_double(self, pieces, got, step):
        return [
            self.double(piece, other, order[step])
            for order, piece, other in zip(self.chip_orders(), pieces, got)
        ]

    def chip_join(self, pieces):
        sides = []
        for order, piece in zip(self.chip_orders(), pieces):
            at = [order[::-1].index(b) for b in sorted(order)[::-1]]
            piece = jnp.transpose(piece, at + list(range(len(at), piece.ndim)))
            sides.append(piece.reshape(-1, piece.shape[-1]))
        return jnp.concatenate(sides, axis=-1)

    def halves(self, part, at, size, mine):
        shape = part.shape
        split = part.reshape(shape[:at] + (shape[at] // (2 * size), 2, size) + shape[at + 1 :])
        rest = shape[:at] + (shape[at] // 2,) + shape[at + 1 :]
        keep = lax.dynamic_index_in_dim(split, mine, at + 1, keepdims=False).reshape(rest)
        give = lax.dynamic_index_in_dim(split, 1 - mine, at + 1, keepdims=False).reshape(rest)
        return keep, give

    def scatter_start(self, value):
        own = value.shape[0] // (self.seqs * self.heads)
        part = value.reshape(self.seqs, self.heads, own, value.shape[1])
        keep, give = self.halves(part, 1, 1, lax.axis_index("head") & 1)
        return keep, self.send(give, self.core)

    def scatter_sides(self, keep, got):
        part = (keep.astype(FLOAT) + got.astype(FLOAT)).astype(LOWER)
        width = part.shape[-1]
        s = lax.axis_index("seq")
        bits = list(range(self.seqs.bit_length() - 1))
        state = []
        for order, piece in (
            (bits, part[..., : width // 2]),
            (bits[::-1], part[..., width // 2 :]),
        ):
            b = order[0]
            keep, give = self.halves(piece, 0, 1 << b, (s >> b) & 1)
            state.append((keep, give, order))
        return state

    def scatter_end(self, state):
        s, h = lax.axis_index("seq"), lax.axis_index("head")
        sides = []
        for keep, got, order in state:
            left = list(order)
            left.remove(order[0])
            piece = (keep.astype(FLOAT) + got.astype(FLOAT)).astype(LOWER)
            for b in order[1:]:
                size = 1 << sorted(left).index(b)
                keep, give = self.halves(piece, 0, size, (s >> b) & 1)
                got = self.send(give, self.swap(1 << b, 0))
                piece = (keep.astype(FLOAT) + got.astype(FLOAT)).astype(LOWER)
                left.remove(b)
            sides.append(piece)
        part = jnp.concatenate(sides, axis=-1)
        for b in range(1, self.heads.bit_length() - 1):
            keep, give = self.halves(part, 1, 1, (h >> b) & 1)
            got = self.send(give, self.swap(0, 1 << b))
            part = (keep.astype(FLOAT) + got.astype(FLOAT)).astype(LOWER)
        return part.reshape(-1, part.shape[-1]).astype(FLOAT)

    def outer_sides(self, block):
        return [self.send(block, self.back(i, 0)) for i in range(1, self.outer_seq)]

    def outer_far(self, block, pieces=1):
        size = block.shape[0] // pieces
        gathered = []
        for j in range(1, self.outer_head):
            got = []
            for p in range(pieces):
                part = block[p * size : (p + 1) * size]
                part = after(part, got[-1]) if got else part
                got.append(self.send(part, self.back(0, j)))
            gathered.append(jnp.concatenate(got) if pieces > 1 else got[0])
        return gathered

    def side_parts(self, parts):
        return [
            self.send(parts[j * self.outer_seq + i], self.ahead(i, 0))
            for j in range(self.outer_head)
            for i in range(1, self.outer_seq)
        ]

    def side_sums(self, parts, got):
        sums = []
        for j in range(self.outer_head):
            here = parts[j * self.outer_seq].astype(FLOAT)
            for i in range(self.outer_seq - 1):
                here = here + got[j * (self.outer_seq - 1) + i].astype(FLOAT)
            sums.append(here if j == 0 else here.astype(LOWER))
        return sums

    def far_parts(self, sums):
        return [self.send(sums[j], self.ahead(0, j)) for j in range(1, self.outer_head)]

    def far_sum(self, sums, got):
        total = sums[0]
        for one in got:
            total = total + one.astype(FLOAT)
        return total

    def corner_gather(self, from_side, from_low):
        half = from_side.shape[0] // 2
        first = self.send(from_side[:half], self.low)
        second = self.send(from_low[half:], self.side)
        return jnp.concatenate([first, second])

    def core_sums(self, parts):
        got = [self.send(one, self.core) for one in parts[4:]]
        return [a.astype(FLOAT) + b.astype(FLOAT) for a, b in zip(parts[:4], got)]

    def corner_sums(self, total):
        corner = total[3].astype(LOWER)
        half = corner.shape[0] // 2
        first = self.send(corner[:half], self.low).astype(FLOAT)
        second = self.send(corner[half:], self.side).astype(FLOAT)
        to_side = jnp.concatenate([total[1][:half] + first, total[1][half:]]).astype(LOWER)
        to_low = jnp.concatenate([total[2][:half], total[2][half:] + second]).astype(LOWER)
        return [total[0], to_side, to_low]

    def near_parts(self, total):
        return [self.send(total[1], self.side), self.send(total[2], self.low)]

    def near_sums(self, total, got):
        return total[0] + got[0].astype(FLOAT) + got[1].astype(FLOAT)

    def outer_owners(self):
        s, h = lax.axis_index("seq"), lax.axis_index("head")
        return [
            ((s + 2 * i) % self.seqs) * self.heads + (h + 4 * j) % self.heads
            for j in range(self.outer_head)
            for i in range(self.outer_seq)
        ]


def body(
    net,
    layer_input,
    mem_count,
    text_len,
    slot_count,
    w_query,
    w_key,
    w_value,
    b_query,
    b_value,
    ln1_gain,
    ln1_bias,
    w_out,
    b_out,
    ln2_gain,
    ln2_bias,
    w_up,
    b_up,
    w_down,
    b_down,
    cotangent,
):
    scale = HEAD_DIM ** (-0.5)
    both = net.axes
    devices = net.seqs * net.heads
    rows, model = layer_input.shape
    width = w_query.shape[1]
    ff_width = w_up.shape[1]
    owners = net.outer_owners()

    small = jnp.concatenate([ln1_gain, ln1_bias, b_out, ln2_gain, ln2_bias, b_down, b_up])
    small = net.row_gather(small)
    own = model // devices

    def vector(i):
        return small[:, i * own : (i + 1) * own].reshape(model).astype(FLOAT)

    gain_one, shift_one, bias_out, gain_two, shift_two, bias_down = [vector(i) for i in range(6)]
    bias_up = jnp.concatenate(
        [lax.dynamic_slice(small, (d, 6 * own), (1, ff_width))[0] for d in owners]
    ).astype(FLOAT)

    core = lax.axis_index("head") & 1
    up_near = [w_up] + net.outer_sides(w_up)
    down_near = [w_down] + net.outer_sides(w_down)
    joint = lax.all_gather(jnp.concatenate([layer_input, w_out]), "head", axis=0)
    cot_side = net.send(cotangent, net.side)
    joint = after(joint, small, cot_side, *up_near, *down_near)
    out_mine = joint.reshape(net.heads // 2, 2, rows + own, model)[:, :, rows:]
    out_mine = lax.dynamic_index_in_dim(out_mine, core, 1, keepdims=False)
    out_pieces = [out_mine[..., : model // 2], out_mine[..., model // 2 :]]
    steps = len(net.chip_orders()[0])
    out_got = net.chip_send(out_pieces, 0)
    up_far = net.outer_far(after(w_up, joint))
    cot_low = net.send(after(cotangent, joint), net.low)
    normed_one, query, keys, values = project(
        joint,
        rows,
        gain_one[None],
        shift_one[None],
        jnp.stack([b_query, b_value]).astype(FLOAT),
        w_query,
        w_key,
        w_value,
    )
    query = after(query, *out_got)
    for step in range(1, steps):
        out_pieces = net.chip_double(out_pieces, [after(one, query) for one in out_got], step - 1)
        out_got = net.chip_send(out_pieces, step)
    counts = jnp.stack([mem_count, text_len, slot_count])
    context, context32, logsum = attention_forward(query, keys, values, counts)
    context = after(context, cot_low, *out_got, *up_far)
    out_pieces = net.chip_double(out_pieces, [after(one, context) for one in out_got], steps - 1)
    out_half = net.chip_join(out_pieces)

    ctx_tok = lax.all_to_all(context, "head", split_axis=0, concat_axis=1, tiled=True)
    cot_corner = net.corner_gather(after(cot_side, context), after(cot_low, context))
    cot_same = [cotangent, cot_side, cot_low, cot_corner]
    cot_blocks = cot_same + [net.send(after(one, context), net.core) for one in cot_same]
    out_other = net.send(after(out_half, context), net.core)
    up_blocks = list(up_near)
    for one in up_far:
        up_blocks += [one] + net.outer_sides(after(one, context))
    down_far = net.outer_far(after(w_down, context), 2)
    ctx_tok = after(ctx_tok, out_other, *up_blocks, *cot_blocks, *down_far)

    inputs_f = layer_input.astype(FLOAT)
    ctx_pairs = ctx_tok.reshape(rows, devices // 2, 2, own)
    ctx_half = lax.dynamic_index_in_dim(ctx_pairs, core, 2, keepdims=False)
    ctx_half = ctx_half.reshape(rows, model // 2)
    ctx_other = lax.dynamic_index_in_dim(ctx_pairs, 1 - core, 2, keepdims=False)
    ctx_other = ctx_other.reshape(rows, model // 2)
    attended = jnp.dot(ctx_half, out_half, preferred_element_type=FLOAT)
    attended = attended + jnp.dot(ctx_other, out_other, preferred_element_type=FLOAT)
    hidden = inputs_f + (attended + bias_out)
    xhat_two, inverse_two = norm_parts(hidden)
    normed_two = (xhat_two * gain_two + shift_two).astype(LOWER)

    cot_group = jnp.concatenate([after(one, normed_two) for one in cot_blocks], axis=0)
    up_full = jnp.concatenate([after(one, normed_two) for one in up_blocks], axis=1)
    n2_side, n2_low = net.send(normed_two, net.side), net.send(normed_two, net.low)
    n2_same = [normed_two, n2_side, n2_low, net.corner_gather(n2_side, n2_low)]
    n2_blocks = n2_same + [net.send(one, net.core) for one in n2_same]
    n2_group = jnp.concatenate(n2_blocks, axis=0)
    down_blocks = list(down_near)
    for one in down_far:
        down_blocks += [one] + net.outer_sides(after(one, ctx_tok))
    n2_group = after(n2_group, *down_blocks)
    down_full = jnp.concatenate([after(one, n2_side) for one in down_blocks], axis=0)
    pre_act = jnp.dot(n2_group, up_full, preferred_element_type=FLOAT) + bias_up
    act, slope = gelu_pair(pre_act)
    act = act.astype(LOWER)
    outer = len(owners)
    down_part = contract_rows(act, cot_group).astype(LOWER)
    down_parts = [down_part[i * ff_width : (i + 1) * ff_width] for i in range(outer)]
    down_got = net.side_parts(down_parts)
    down_later = after(down_full, down_part)
    out_part = jnp.dot(act, down_later, preferred_element_type=FLOAT).astype(LOWER)
    sums_out = net.core_sums([out_part[i * rows : (i + 1) * rows] for i in range(8)])
    grad_pre = (slope * cols_by_cols(after(cot_group, out_part), down_later)).astype(LOWER)
    out_stage = net.corner_sums(sums_out)
    out_near = net.near_parts(out_stage)
    up_later = after(up_full, *down_got[1::2])
    grad_n2_part = cols_by_cols(grad_pre, up_later).astype(LOWER)
    sums_n2 = net.core_sums([grad_n2_part[i * rows : (i + 1) * rows] for i in range(8)])
    up_part = contract_rows(n2_group, after(grad_pre, grad_n2_part, *out_stage[1:])).astype(LOWER)
    sums_n2[3] = after(sums_n2[3], up_part, *out_near)
    out_sum = net.near_sums(out_stage, out_near)
    down_sums = net.side_sums(down_parts, down_got)
    down_far_got = net.far_parts(down_sums)
    n2_stage = net.corner_sums(sums_n2)
    up_parts = [up_part[:, i * ff_width : (i + 1) * ff_width] for i in range(outer)]
    up_got = net.side_parts(up_parts)
    n2_stage[1] = after(n2_stage[1], *up_got[1::2], *down_far_got)
    n2_stage[2] = after(n2_stage[2], n2_stage[1])
    grad_n2 = net.near_sums(n2_stage, net.near_parts(n2_stage))
    grad_n2 = after(grad_n2, *up_got[::2], *down_got[::2])
    grad_w_down = net.far_sum(down_sums, [after(one, grad_n2) for one in down_far_got])
    half = model // 2
    up_sums = net.side_sums(up_parts, [after(one, grad_n2) for one in up_got])
    up_halves = [[one[:half] for one in up_sums], [one[half:] for one in up_sums]]
    up_far_got = net.far_parts(up_halves[0])
    b_up_part = jnp.sum(grad_pre.astype(FLOAT), 0)

    grad_out_f = cotangent.astype(FLOAT)
    b_down_part = jnp.sum(grad_out_f, 0)
    gain_two_part = jnp.sum(grad_n2 * xhat_two, 0)
    shift_two_part = jnp.sum(grad_n2, 0)
    grad_hidden = grad_out_f + norm_back(xhat_two, inverse_two, gain_two, grad_n2)
    grad_att = grad_hidden.astype(LOWER)
    b_out_part = jnp.sum(grad_att.astype(FLOAT), 0)
    grad_ctx = jnp.stack(
        [cols_by_cols(grad_att, one).reshape(rows, devices // 2, own) for one in (out_half, out_other)],
        axis=2,
    )
    grad_ctx = jnp.where(core == 0, grad_ctx, grad_ctx[:, :, ::-1]).astype(LOWER)
    grad_ctx = grad_ctx.reshape(rows, model)
    grad_heads = lax.all_to_all(grad_ctx, "head", split_axis=1, concat_axis=0, tiled=True)

    out_keep, out_got = net.scatter_start(contract_rows(ctx_tok, grad_att).astype(LOWER))
    out_state = net.scatter_sides(out_keep, out_got)
    grad_heads = after(grad_heads, *up_far_got, *[give for _, give, _ in out_state])
    up_far_late = net.far_parts([after(one, grad_heads) for one in up_halves[1]])
    out_state = [(k, after(g, grad_heads), o) for k, g, o in out_state]
    out_state = [(k, net.send(g, net.swap(1 << o[0], 0)), o) for k, g, o in out_state]

    grad_q, grad_k, grad_v = attention_backward(
        query, keys, values, context32, grad_heads, logsum, counts
    )
    grad_joined = jnp.concatenate([grad_q, grad_k, grad_v], axis=1)
    out_raw = [got for _, got, _ in out_state]
    grad_joined = after(grad_joined, *out_raw, *up_far_late)
    output = (hidden + (out_sum + bias_down)).astype(LOWER)
    out_state = [(k, after(g, grad_joined), o) for k, g, o in out_state]
    grad_w_up = jnp.concatenate(
        [
            net.far_sum(sums, [after(one, grad_joined) for one in got])
            for sums, got in zip(up_halves, (up_far_got, up_far_late))
        ]
    )
    joined_w = jnp.concatenate([w_query, w_key, w_value], axis=1)
    grad_n1_part = cols_by_cols(grad_joined, joined_w).astype(LOWER)
    weight_part = contract_rows(normed_one, after(grad_joined, grad_n1_part)).astype(LOWER)
    grad_n1 = lax.psum_scatter(grad_n1_part, "head", scatter_dimension=0, tiled=True).astype(FLOAT)
    up_rows = jnp.zeros((devices, ff_width), FLOAT)
    for i, owner in enumerate(owners):
        up_rows = lax.dynamic_update_slice(
            up_rows, b_up_part[i * ff_width : (i + 1) * ff_width][None], (owner, 0)
        )
    early_rows = (
        jnp.concatenate(
            [
                part.reshape(devices, own)
                for part in (b_out_part, gain_two_part, shift_two_part, b_down_part)
            ]
            + [up_rows],
            axis=1,
        )
    )
    early = net.row_scatter(after(early_rows, grad_n1_part))
    weight_part = after(weight_part, early)
    weight_sum = net.seq_sum(weight_part)
    late_gate = weight_sum
    weight_sum = weight_sum.astype(FLOAT)
    weight_sum = [weight_sum[:, i * width : (i + 1) * width] for i in range(3)]
    grad_w_out = net.scatter_end(out_state)
    grad_n1 = after(grad_n1, *weight_sum, grad_w_up, grad_w_out)
    b_query_part = jnp.sum(grad_q.astype(FLOAT), 0)
    b_value_part = jnp.sum(grad_v.astype(FLOAT), 0)

    xhat_one, inverse_one = norm_parts(inputs_f)
    n1_part, x_group, _ = lax.optimization_barrier((grad_n1_part, joint, weight_part))
    x_group = x_group[:, :rows].reshape(-1, model)
    n1_part = n1_part.astype(FLOAT)
    xhat_all, _ = norm_parts(x_group.astype(FLOAT))
    gain_one_part = jnp.sum(n1_part * xhat_all, 0)
    shift_one_part = jnp.sum(n1_part, 0)
    grad_input = (grad_hidden + norm_back(xhat_one, inverse_one, gain_one, grad_n1)).astype(LOWER)

    row_of = jnp.arange(devices, dtype=jnp.int32)
    mine = (row_of % net.heads == lax.axis_index("head"))[:, None]
    head_rows = jnp.where(mine, jnp.concatenate([b_query_part, b_value_part])[None], 0.0)
    late_rows = jnp.concatenate(
        [part.reshape(devices, own) for part in (gain_one_part, shift_one_part)] + [head_rows],
        axis=1,
    )
    late = net.row_scatter(after(late_rows, late_gate))
    pieces = [late[:own], late[own : 2 * own]] + [early[i * own : (i + 1) * own] for i in range(4)]
    grad_b_up = early[4 * own :]
    grad_b_query = late[2 * own : 2 * own + width]
    grad_b_value = late[2 * own + width :]

    return (
        output,
        grad_input,
        weight_sum[0],
        weight_sum[1],
        weight_sum[2],
        grad_b_query,
        grad_b_value,
        pieces[0],
        pieces[1],
        grad_w_out,
        pieces[2],
        pieces[3],
        pieces[4],
        grad_w_up,
        grad_b_up,
        grad_w_down,
        pieces[5],
    )


def solution(mesh):
    net = Exchange(mesh.shape["seq"], mesh.shape["head"])
    rows = P(("seq", "head"), None)
    cols = P(None, ("seq", "head"))
    vec = P(("seq", "head"))
    head_cols = P(None, "head")
    head_vec = P("head")
    count = P("seq")
    return jax.shard_map(
        functools.partial(body, net),
        mesh=mesh,
        in_specs=(
            rows,
            count,
            count,
            count,
            head_cols,
            head_cols,
            head_cols,
            head_vec,
            head_vec,
            vec,
            vec,
            rows,
            vec,
            vec,
            vec,
            cols,
            vec,
            rows,
            vec,
            rows,
        ),
        out_specs=(
            rows,
            rows,
            head_cols,
            head_cols,
            head_cols,
            head_vec,
            head_vec,
            vec,
            vec,
            rows,
            vec,
            vec,
            vec,
            cols,
            vec,
            rows,
            vec,
        ),
        check_vma=False,
    )
```
